32 devices in a mesh: groups: 2 (over x), coarse: 16 (over z, y, core).
Axes of the slice: x: 2, y: 2, z: 4, core: 2. Of those that a mesh axis runs over, the one named last changes fastest.
Arguments:
- fine_feats: bfloat16 [49152, 256], P(('groups', 'coarse')), parts along dimension 0, may hold values from -60 to 60
- down_weight: bfloat16 [8, 256, 512], replicated, may hold values from -0.125 to 0.125
- gain: float32 [512], replicated, may hold values from 0.1 to 1.9
- shift: float32 [512], replicated, may hold values from -1 to 1
- subm_weight: bfloat16 [27, 512, 256], replicated, may hold values from -0.078125 to 0.078125
- child: int32 [16, 6144], P('groups', 'coarse'), parts along dimension 0, may hold values from 0 to 1536, as said below
- live: int32 [32], P(('groups', 'coarse')), parts along dimension 0, may hold values from 128 to 384, as said below
- send_rows: int32 [8, 1024], P('groups', 'coarse'), parts along dimension 0, may hold values from 0 to 383, as said below
- nbr: int32 [54, 6144], P('groups', 'coarse'), parts along dimension 0, may hold values from 0 to 640, as said below
- grad_out: bfloat16 [12288, 256], P(('groups', 'coarse')), parts along dimension 0, may hold values from -8 to 8
Outputs:
- features_out: bfloat16 [12288, 256], P(('groups', 'coarse')), parts along dimension 0
- grad_fine: bfloat16 [49152, 256], P(('groups', 'coarse')), parts along dimension 0
- grad_down: bfloat16 [16, 256, 512], P('groups'), parts along dimension 0
- grad_gain: float32 [1024], P('groups'), parts along dimension 0
- grad_shift: float32 [1024], P('groups'), parts along dimension 0
The draws below stay inside these ranges and needn't reach their ends.
There are 2 independent parts, one for each index of `groups`. The reference program is written for one: setup_inputs(seed, part) draws one part's arguments, and reference() takes and returns one part's arrays. A program takes and returns all parts, laid end to end along the dimension named above; an argument that names none is the same for every part. Nothing has to cross between parts.
Inputs may be any that keep to these rules, and one draw needn't show every extreme that they name: Within each block, every fine row 0..1535 is the child of exactly one (k, p); 1536 marks a missing child. `live`: some block is full in every draw. `send_rows`: entry [j, b*64 + i] is a local row of block b. `nbr`: indexes the table of the row's own block; entry 640 is the zero row and occurs; entry k = 13 is the row itself.
All inputs are finite; a program needn't handle non-finite values.
Results may differ from the reference program's by a relative error of at most 0.0059.
Values may be sent and summed in bfloat16 or wider, within the bound.
A program may use at most 128 MiB of HBM per device.

```python
import math
import jax
import jax.numpy as jnp
from jax import lax

CIN = 256
C = 512
CO = 256
KD = 8
KS = 27
NDIR = 4
HALO = 64
R16_DEV = 384
R8_DEV = 1536
COARSE = 6144
FINE = 24576
N_COARSE = 16


def draw_fine_feats(key, part):
    key = jax.random.fold_in(key, 11)
    key_base = jax.random.fold_in(key, 0)
    key_cols = jax.random.fold_in(key, 2)
    rise_rows = 1.0 + 2.0 * jnp.arange(FINE, dtype=jnp.float32)[:, None] / FINE
    base_draw = jax.random.normal(key_base, (FINE, CIN), jnp.float32)
    col_scale = jnp.exp(jax.random.uniform(key_cols, (1, CIN), jnp.float32, 0.0, math.log(3.0)))
    values = base_draw * rise_rows * col_scale
    return jnp.clip(values, -60.0, 60.0).astype(jnp.bfloat16)


def draw_child(key, part):
    key = jax.random.fold_in(key, 12)
    blocks = COARSE // R16_DEV
    block_keys = jax.random.split(key, blocks)
    shuffled = jax.vmap(lambda block_key: jax.random.permutation(block_key, KD * R16_DEV))(block_keys)
    slot_rows = jnp.where(shuffled < R8_DEV, shuffled, R8_DEV).astype(jnp.int32)
    return slot_rows.reshape(blocks, R16_DEV, KD).transpose(2, 0, 1).reshape(KD, COARSE)


def draw_live(key, part):
    key = jax.random.fold_in(key, 13)
    key_counts, key_full = jax.random.split(key)
    blocks = COARSE // R16_DEV
    counts = jax.random.randint(key_counts, (blocks,), R16_DEV // 3, R16_DEV + 1)
    full_block = jax.random.randint(key_full, (), 0, blocks)
    return jnp.where(jnp.arange(blocks) == full_block, R16_DEV, counts).astype(jnp.int32)


def draw_send_rows(key, part):
    key = jax.random.fold_in(key, 14)
    return jax.random.randint(key, (NDIR, COARSE // R16_DEV * HALO), 0, R16_DEV).astype(jnp.int32)


def draw_nbr(key, part):
    key = jax.random.fold_in(key, 15)
    key_kind, key_local, key_remote = jax.random.split(key, 3)
    category = jax.random.randint(key_kind, (KS, COARSE), 0, 20)
    local_row = jax.random.randint(key_local, (KS, COARSE), 0, R16_DEV)
    remote = R16_DEV + jax.random.randint(key_remote, (KS, COARSE), 0, NDIR * HALO)
    absent = R16_DEV + NDIR * HALO
    table_ids = jnp.where(category < 6, local_row, jnp.where(category < 8, remote, absent))
    own_row = jnp.arange(COARSE, dtype=jnp.int32) % R16_DEV
    table_ids = jnp.where(jnp.arange(KS)[:, None] == KS // 2, own_row[None, :], table_ids)
    table_ids = table_ids.at[0, 0].set(absent)
    return table_ids.astype(jnp.int32)


def draw_grad_out(key, part):
    key = jax.random.fold_in(key, 16)
    key_base, key_offset = jax.random.split(key, 2)
    rise_rows = 1.0 + 2.0 * jnp.arange(COARSE, dtype=jnp.float32)[:, None] / COARSE
    channel_offset = jax.random.normal(key_offset, (1, CO), jnp.float32)
    base_draw = jax.random.normal(key_base, (COARSE, CO), jnp.float32)
    values = base_draw + 0.5 * channel_offset * rise_rows
    return jnp.clip(values, -8.0, 8.0).astype(jnp.bfloat16)


def gaussian(own_key, shape, spread, most, kind=jnp.bfloat16):
    return jnp.clip(spread * jax.random.normal(own_key, shape, jnp.float32), -most, most).astype(kind)


def setup_inputs(seed: int = 0, part: int = 0) -> dict:
    arg_keys = jax.random.split(jax.random.key(seed), 11)
    part_keys = jax.random.split(jax.random.fold_in(arg_keys[10], part), 11)
    return {
        "fine_feats": draw_fine_feats(jax.random.fold_in(jax.random.fold_in(arg_keys[10], part), 71), part),
        "down_weight": gaussian(arg_keys[1], (KD, CIN, C), (KD * CIN) ** -0.5, 0.125),
        "gain": jnp.clip(1.0 + 0.18 * jax.random.normal(arg_keys[2], (C,), jnp.float32), 0.1, 1.9),
        "shift": jnp.clip(jax.random.uniform(arg_keys[3], (C,), jnp.float32, -1.0, 1.0), -1.0, 1.0),
        "subm_weight": gaussian(arg_keys[4], (KS, C, CO), (11 * C) ** -0.5, 0.078125),
        "child": draw_child(jax.random.fold_in(jax.random.fold_in(arg_keys[10], part), 71), part),
        "live": draw_live(jax.random.fold_in(jax.random.fold_in(arg_keys[10], part), 71), part),
        "send_rows": draw_send_rows(jax.random.fold_in(jax.random.fold_in(arg_keys[10], part), 71), part),
        "nbr": draw_nbr(jax.random.fold_in(jax.random.fold_in(arg_keys[10], part), 71), part),
        "grad_out": draw_grad_out(jax.random.fold_in(jax.random.fold_in(arg_keys[10], part), 71), part),
    }


OFFSETS = (1, 2, -1, -2)
EPSILON = 1e-05

def silu_parts(hidden):
    sigmoid_v = 1.0 / (1.0 + jnp.exp(-hidden))
    return (hidden * sigmoid_v, sigmoid_v * (1.0 + hidden * (1.0 - sigmoid_v)))

def move_blocks(blocks, offset):
    zeros_part = jnp.zeros_like(blocks[:abs(offset)])
    if offset > 0:
        return jnp.concatenate([zeros_part, blocks[:-offset]], 0)
    return jnp.concatenate([blocks[-offset:], zeros_part], 0)

def take_rows(tables, index):
    return jax.vmap(lambda table_b, index_b: table_b[index_b])(tables, index)

def add_rows(grads, index, values):
    return jax.vmap(lambda grads_b, index_b, values_b: grads_b.at[index_b].add(values_b))(grads, index, values)

def reference(fine_feats, down_weight, gain, shift, subm_weight, child, live, send_rows, nbr, grad_out):
    blocks = N_COARSE
    fine_blocks = jnp.concatenate([fine_feats.reshape(blocks, R8_DEV, CIN), jnp.zeros((blocks, 1, CIN), jnp.bfloat16)], 1)
    child_b = child.reshape(KD, blocks, R16_DEV).transpose(1, 2, 0)
    gathered = take_rows(fine_blocks, child_b).reshape(COARSE, KD * CIN)
    flat_down = down_weight.reshape(KD * CIN, C)
    conv_out = jnp.dot(gathered, flat_down, preferred_element_type=jnp.float32).astype(jnp.bfloat16)
    conv_wide = lax.optimization_barrier(conv_out).astype(jnp.float32)
    row_mask = (jnp.arange(R16_DEV, dtype=jnp.int32)[None, :] < live[:, None]).astype(jnp.float32).reshape(COARSE, 1)
    filled = jnp.sum(live.astype(jnp.float32))
    mean_row = lax.optimization_barrier(jnp.sum(row_mask * conv_wide, 0)) / filled
    centred = conv_wide - mean_row
    variance = lax.optimization_barrier(jnp.sum(row_mask * centred * centred, 0)) / filled
    inv_std = lax.rsqrt(variance + EPSILON)
    normed = centred * inv_std
    hidden = normed * gain + shift
    activated, silu_slope = silu_parts(hidden)
    active = (row_mask * activated).astype(jnp.bfloat16)
    active_b = active.reshape(blocks, R16_DEV, C)
    send_b = send_rows.reshape(NDIR, blocks, HALO)
    pieces = [active_b]
    for slot_j in range(NDIR):
        pieces.append(move_blocks(take_rows(active_b, send_b[slot_j]), OFFSETS[slot_j]))
    pieces.append(jnp.zeros((blocks, 1, C), jnp.bfloat16))
    table_ext = jnp.concatenate(pieces, 1)
    extent = R16_DEV + NDIR * HALO + 1
    nbr_k = nbr.reshape(KS, blocks, R16_DEV)

    def forward_step(summed, inputs):
        index_k, weight_k = inputs
        rows_k = take_rows(table_ext, index_k).reshape(COARSE, C)
        return (summed + jnp.dot(rows_k, weight_k, preferred_element_type=jnp.float32), None)
    summed, unused = lax.scan(forward_step, jnp.zeros((COARSE, CO), jnp.float32), (nbr_k, subm_weight))
    features_out = summed.astype(jnp.bfloat16)
    base_index = (jnp.arange(blocks, dtype=jnp.int32) * extent)[:, None]

    def backward_step(table_grad, inputs):
        index_k, weight_k = inputs
        contrib = lax.dot_general(grad_out, weight_k, (((1,), (1,)), ((), ())), preferred_element_type=jnp.float32)
        return (table_grad.at[(base_index + index_k).reshape(-1)].add(contrib), None)
    table_grad, unused = lax.scan(backward_step, jnp.zeros((blocks * extent, C), jnp.float32), (nbr_k, subm_weight))
    table_grad = table_grad.reshape(blocks, extent, C)
    grad_active = table_grad[:, :R16_DEV]
    for slot_j in range(NDIR):
        start_j = R16_DEV + slot_j * HALO
        returned = move_blocks(table_grad[:, start_j:start_j + HALO], -OFFSETS[slot_j])
        grad_active = add_rows(grad_active, send_b[slot_j], returned)
    grad_active = grad_active.reshape(COARSE, C)
    grad_hidden = row_mask * grad_active * silu_slope
    grad_gain = lax.optimization_barrier(jnp.sum(grad_hidden * normed, 0))
    grad_shift = lax.optimization_barrier(jnp.sum(grad_hidden, 0))
    grad_pre = (row_mask * gain * inv_std * (grad_hidden - (grad_shift + normed * grad_gain) / filled)).astype(jnp.bfloat16)
    grad_down = lax.dot_general(gathered, grad_pre, (((0,), (0,)), ((), ())), preferred_element_type=jnp.float32)
    grad_down = grad_down.astype(jnp.bfloat16).reshape(KD, CIN, C)
    spread_down = lax.dot_general(grad_pre, flat_down, (((1,), (1,)), ((), ())), preferred_element_type=jnp.float32)
    spread_down = spread_down.reshape(blocks, R16_DEV * KD, CIN)
    fine_grad = add_rows(jnp.zeros((blocks, R8_DEV + 1, CIN), jnp.float32), child_b.reshape(blocks, R16_DEV * KD), spread_down)
    grad_fine = fine_grad[:, :R8_DEV].reshape(FINE, CIN).astype(jnp.bfloat16)
    return (features_out, grad_fine, grad_down, grad_gain, grad_shift)
```

```python
import functools

import jax
import jax.numpy as jnp
from jax import lax
from jax.experimental import pallas as pl
from jax.experimental.pallas import tpu as pltpu
from jax.sharding import PartitionSpec as P

OFFSETS = (1, 2, -1, -2)
EPSILON = 1e-05
LANES = 2
F32 = jnp.float32
BF16 = jnp.bfloat16
MESH = pl.DeviceIdType.MESH


def silu_parts(hidden):
    sigmoid_v = 1.0 / (1.0 + jnp.exp(-hidden))
    return (hidden * sigmoid_v, sigmoid_v * (1.0 + hidden * (1.0 - sigmoid_v)))


def pick_rows(column, size):
    wide = lax.broadcasted_iota(jnp.int32, (column.shape[0], size), 1)
    return jnp.where(wide == column, 1.0, 0.0).astype(BF16)


def drop_rows(row, size):
    tall = lax.broadcasted_iota(jnp.int32, (size, row.shape[1]), 0)
    return jnp.where(tall == row, 1.0, 0.0).astype(BF16)


def as_column(row):
    return jnp.transpose(jnp.broadcast_to(row, (8, row.shape[1])))[:, :1]


def dot(a, b, ca=1, cb=0):
    return lax.dot_general(a, b, (((ca,), (cb,)), ((), ())), preferred_element_type=F32)


def kernel(
    n, fine, wd_hbm, gain, shift, ws_hbm, child, live, send_rows, nbr, gout,
    feat_o, fine_o, down_o, gain_o, shift_o,
    wd, ws, gath, conv, table, tgrad, facc, gpre, dspread, part,
    sbuf, rbuf, obuf, st1, st2, hsend, hrecv, bsend, brecv,
    wsem, s1s, s1r, s2s, s2r, hss, hsr, bss, bsr, rss, rsr, ags, agr,
):
    kd, cin, c = wd.shape
    ks, _, co = ws.shape
    rows = child.shape[1]
    ndir, halo = send_rows.shape
    fine_rows = fine.shape[0]
    ext = rows + ndir * halo
    q_count, total, width = part.shape
    me = lax.axis_index("coarse")

    wd_copy = pltpu.make_async_copy(wd_hbm, wd, wsem.at[0])
    ws_copy = pltpu.make_async_copy(ws_hbm, ws, wsem.at[1])
    wd_copy.start()
    ws_copy.start()

    barrier = pltpu.get_barrier_semaphore()

    @pl.loop(1, n)
    def _(d):
        pl.semaphore_signal(barrier, inc=1, device_id={"coarse": lax.rem(me + d, n)}, device_id_type=MESH)

    def remote(src, dst, ssem, rsem, to):
        return pltpu.make_async_remote_copy(
            src_ref=src, dst_ref=dst, send_sem=ssem, recv_sem=rsem,
            device_id={"coarse": to}, device_id_type=MESH,
        )

    def tell_all(st, ss, sr):
        @pl.loop(1, n)
        def _(d):
            remote(st.at[me], st.at[me], ss.at[d], sr.at[me], lax.rem(me + d, n)).start()

    def hear_all(st, ss, sr):
        @pl.loop(1, n)
        def _(d):
            src = lax.rem(me - d + n, n)
            remote(st.at[src], st.at[src], ss.at[d], sr.at[src], lax.rem(me + d, n)).wait()

    conv[...] = jnp.zeros_like(conv)
    wd_copy.wait()

    @pl.loop(0, kd)
    def _(k):
        sel = pick_rows(as_column(child[pl.ds(k, 1), :]), fine_rows)
        g = dot(sel, fine[...]).astype(BF16)
        gath[k] = g
        conv[...] += dot(g, wd[k])

    wide = conv[...].astype(BF16).astype(F32)
    conv[...] = wide
    row_mask = (lax.broadcasted_iota(jnp.int32, (rows, 1), 0) < live[0]).astype(F32)
    masked = row_mask * wide
    sums = jnp.sum(masked, 0, keepdims=True)
    squares = jnp.sum(masked * wide, 0, keepdims=True)
    pieces = c // 128
    for r in range(pieces):
        st1[me, r : r + 1, :] = sums[:, r * 128 : (r + 1) * 128]
        st1[me, pieces + r : pieces + r + 1, :] = squares[:, r * 128 : (r + 1) * 128]
    live_count = jnp.full((8, 128), live[0], jnp.int32).astype(F32)
    st1[me, 2 * pieces : 2 * pieces + 8, :] = live_count
    pl.semaphore_wait(barrier, n - 1)
    tell_all(st1, s1s, s1r)

    tgrad[...] = jnp.zeros_like(tgrad)
    ws_copy.wait()

    @pl.loop(0, ks // 3)
    def _(k3):
        total_k = None
        for i in range(3):
            k = k3 * 3 + i
            spread = dot(drop_rows(nbr[pl.ds(k, 1), :], ext), gout[...]).astype(BF16)
            term = dot(spread, ws[k], 1, 1)
            total_k = term if total_k is None else total_k + term
        tgrad[...] += total_k

    def back_copy(j):
        return remote(
            bsend.at[j], brecv.at[j], bss.at[j], bsr.at[j], lax.rem(me - OFFSETS[j] + n, n)
        )

    def halo_copy(j):
        return remote(
            hsend.at[j], hrecv.at[j], hss.at[j], hsr.at[j], lax.rem(me + OFFSETS[j] + n, n)
        )

    for j in range(ndir):
        bsend[j] = tgrad[rows + j * halo : rows + (j + 1) * halo, :].astype(BF16)
        back_copy(j).start()

    hear_all(st1, s1s, s1r)

    def add_slots(st):
        acc = st[0]
        for i in range(1, n):
            acc = acc + st[i]
        return acc

    def flat(acc, first):
        return jnp.concatenate([acc[first + r : first + r + 1, :] for r in range(pieces)], 1)

    acc1 = add_slots(st1)
    filled = acc1[2 * pieces : 2 * pieces + 1, :1]
    mean = flat(acc1, 0) / filled
    variance = flat(acc1, pieces) / filled - mean * mean
    inv_std = lax.rsqrt(variance + EPSILON)
    normed = (conv[...] - mean) * inv_std
    hidden = normed * gain[...] + shift[...]
    activated, slope = silu_parts(hidden)
    active = (row_mask * activated).astype(BF16)
    table[:rows, :] = active
    conv[...] = normed
    for j in range(ndir):
        sel = drop_rows(send_rows[j : j + 1, :], rows)
        hsend[j] = dot(sel, active, 0, 0).astype(BF16)
        halo_copy(j).start()

    grad_active = tgrad[:rows, :]
    for j in range(ndir):
        back_copy(j).wait()
        giver = me + OFFSETS[j]
        there = jnp.logical_and(giver >= 0, giver < n)
        back = jnp.where(there, brecv[j], jnp.zeros_like(brecv[j]))
        grad_active = grad_active + dot(drop_rows(send_rows[j : j + 1, :], rows), back)
    grad_hidden = row_mask * grad_active * slope
    tgrad[:rows, :] = grad_hidden
    part_gain = jnp.sum(grad_hidden * normed, 0, keepdims=True)
    part_shift = jnp.sum(grad_hidden, 0, keepdims=True)
    for r in range(pieces):
        st2[me, r : r + 1, :] = part_gain[:, r * 128 : (r + 1) * 128]
        st2[me, pieces + r : pieces + r + 1, :] = part_shift[:, r * 128 : (r + 1) * 128]
    tell_all(st2, s2s, s2r)

    for j in range(ndir):
        halo_copy(j).wait()
        giver = me - OFFSETS[j]
        there = jnp.logical_and(giver >= 0, giver < n)
        table[rows + j * halo : rows + (j + 1) * halo, :] = jnp.where(
            there, hrecv[j], jnp.zeros_like(hrecv[j])
        )
    facc[...] = jnp.zeros_like(facc)

    def forward(first, last):
        @pl.loop(first, last)
        def _(k):
            sel = pick_rows(as_column(nbr[pl.ds(k, 1), :]), ext)
            facc[...] += dot(dot(sel, table[...]).astype(BF16), ws[k])

    forward(0, 3)

    hear_all(st2, s2s, s2r)
    acc2 = add_slots(st2)
    grad_gain = flat(acc2, 0)
    grad_shift = flat(acc2, pieces)
    gain_o[...] = grad_gain
    shift_o[...] = grad_shift
    gpre[...] = (
        row_mask * gain[...] * inv_std
        * (tgrad[:rows, :] - (grad_shift + conv[...] * grad_gain) / filled)
    ).astype(BF16)

    masks = []
    while 2 ** len(masks) < n:
        masks.append(2 ** len(masks))
    steps = len(masks)
    lows, sends, partners, lengths, places = [], [], [], [], []
    low, length, place = 0, total, 0
    for m in masks:
        bit = lax.rem(me // m, 2)
        length = length // 2
        lengths.append(length)
        sends.append(pl.multiple_of(low + (1 - bit) * length, length))
        low = low + bit * length
        lows.append(pl.multiple_of(low, length))
        partners.append(me + m - 2 * m * bit)
        places.append(place)
        place += length

    def sum_copy(q, s):
        span = pl.ds(places[s], lengths[s])
        return remote(
            sbuf.at[q, span], rbuf.at[q, span], rss.at[q, s], rsr.at[q, s], partners[s]
        )

    def full_copy(q, s):
        span = pl.ds(lows[s], lengths[s])
        return remote(
            obuf.at[q, span], obuf.at[q, span], ags.at[q, s], agr.at[q, s], partners[s]
        )

    def start(q, t):
        if t < steps:
            sbuf[q, places[t] : places[t] + lengths[t], :] = part[
                q, pl.ds(sends[t], lengths[t]), :
            ].astype(BF16)
            sum_copy(q, t).start()
        elif t < 2 * steps:
            full_copy(q, 2 * steps - 1 - t).start()

    def finish(q, t):
        if t < steps:
            sum_copy(q, t).wait()
            span = pl.ds(lows[t], lengths[t])
            summed = part[q, span, :] + rbuf[q, places[t] : places[t] + lengths[t], :].astype(F32)
            if t < steps - 1:
                part[q, span, :] = summed
            else:
                obuf[q, span, :] = summed.astype(BF16)
        else:
            full_copy(q, 2 * steps - 1 - t).wait()

    for q in range(q_count):
        @pl.loop(0, kd)
        def _(k):
            part[q, pl.ds(pl.multiple_of(k * cin, cin), cin), :] = dot(
                gath[k], gpre[:, q * width : (q + 1) * width], 0, 0
            )

        start(q, 0)

    def spread_down():
        @pl.loop(0, kd)
        def _(k):
            dspread[pl.ds(pl.multiple_of(k * rows, rows), rows), :] = dot(
                gpre[...], wd[k], 1, 1
            ).astype(BF16)

    tile = 256

    def fine_tiles(first, last):
        @pl.loop(first, last)
        def _(i):
            base = pl.multiple_of(i * tile, tile)
            acc = jnp.zeros((tile, cin), F32)
            for k in range(kd):
                sel = drop_rows(child[k : k + 1, :] - base, tile)
                acc = acc + dot(sel, dspread[k * rows : (k + 1) * rows, :])
            fine_o[pl.ds(base, tile), :] = acc.astype(BF16)

    units = [functools.partial(forward, k, min(k + 2, ks)) for k in range(3, ks, 2)]
    units.append(spread_down)
    tiles = fine_rows // tile
    units += [functools.partial(fine_tiles, i, i + 1) for i in range(tiles)]
    for t in range(2 * steps):
        for q in range(q_count):
            finish(q, t)
            start(q, t + 1)
            if units:
                units.pop(0)()
    for unit in units:
        unit()
    feat_o[...] = facc[...].astype(BF16)
    for q in range(q_count):
        down_o[:, q * width : (q + 1) * width] = obuf[q]


def body(fine_feats, down_weight, gain, shift, subm_weight, child, live, send_rows, nbr, grad_out):
    n = lax.axis_size("coarse")
    fine_rows, cin = fine_feats.shape
    kd, _, c = down_weight.shape
    ks, _, co = subm_weight.shape
    rows = child.shape[1]
    ndir, halo = send_rows.shape
    ext = rows + ndir * halo
    width = c // LANES
    total = kd * cin
    steps = max(1, (n - 1).bit_length())
    slot = 2 * (c // 128)
    vmem = pl.BlockSpec(memory_space=pltpu.VMEM)
    hbm = pl.BlockSpec(memory_space=pl.ANY)
    smem = pl.BlockSpec(memory_space=pltpu.SMEM)
    dma = pltpu.SemaphoreType.DMA
    features, grad_fine, grad_down, grad_gain, grad_shift = pl.pallas_call(
        functools.partial(kernel, n),
        out_shape=(
            jax.ShapeDtypeStruct((rows, co), BF16),
            jax.ShapeDtypeStruct((fine_rows, cin), BF16),
            jax.ShapeDtypeStruct((total, c), BF16),
            jax.ShapeDtypeStruct((1, c), F32),
            jax.ShapeDtypeStruct((1, c), F32),
        ),
        in_specs=[vmem, hbm, vmem, vmem, hbm, vmem, smem, vmem, vmem, vmem],
        out_specs=(vmem,) * 5,
        scratch_shapes=[
            pltpu.VMEM((kd, cin, c), BF16),
            pltpu.VMEM((ks, c, co), BF16),
            pltpu.VMEM((kd, rows, cin), BF16),
            pltpu.VMEM((rows, c), F32),
            pltpu.VMEM((ext, c), BF16),
            pltpu.VMEM((ext, c), F32),
            pltpu.VMEM((rows, co), F32),
            pltpu.VMEM((rows, c), BF16),
            pltpu.VMEM((kd * rows, cin), BF16),
            pltpu.VMEM((LANES, total, width), F32),
            pltpu.VMEM((LANES, total, width), BF16),
            pltpu.VMEM((LANES, total, width), BF16),
            pltpu.VMEM((LANES, total, width), BF16),
            pltpu.VMEM((n, slot + 8, 128), F32),
            pltpu.VMEM((n, slot, 128), F32),
            pltpu.VMEM((ndir, halo, c), BF16),
            pltpu.VMEM((ndir, halo, c), BF16),
            pltpu.VMEM((ndir, halo, c), BF16),
            pltpu.VMEM((ndir, halo, c), BF16),
            dma((2,)),
            dma((n,)), dma((n,)), dma((n,)), dma((n,)),
            dma((ndir,)), dma((ndir,)), dma((ndir,)), dma((ndir,)),
            dma((LANES, steps)), dma((LANES, steps)), dma((LANES, steps)), dma((LANES, steps)),
        ],
        compiler_params=pltpu.CompilerParams(
            collective_id=0, has_side_effects=True, vmem_limit_bytes=56 * 1024 * 1024
        ),
    )(
        fine_feats, down_weight, gain.reshape(1, c), shift.reshape(1, c), subm_weight,
        child, live, send_rows, nbr, grad_out,
    )
    return (
        features,
        grad_fine,
        grad_down.reshape(kd, cin, c),
        grad_gain.reshape(c),
        grad_shift.reshape(c),
    )


def solution(mesh):
    in_specs = (
        P(("groups", "coarse"), None),
        P(),
        P(),
        P(),
        P(),
        P("groups", "coarse"),
        P(("groups", "coarse")),
        P("groups", "coarse"),
        P("groups", "coarse"),
        P(("groups", "coarse"), None),
    )
    out_specs = (
        P(("groups", "coarse"), None),
        P(("groups", "coarse"), None),
        P("groups", None, None),
        P("groups"),
        P("groups"),
    )
    return jax.shard_map(body, mesh=mesh, in_specs=in_specs, out_specs=out_specs, check_vma=False)
```

```python
import functools

import jax
import jax.numpy as jnp
from jax import lax
from jax.experimental import pallas as pl
from jax.experimental.pallas import tpu as pltpu
from jax.sharding import PartitionSpec as P

OFFSETS = (1, 2, -1, -2)
EPSILON = 1e-05
LANES = 4
F32 = jnp.float32
BF16 = jnp.bfloat16
MESH = pl.DeviceIdType.MESH


def silu_parts(hidden):
    sigmoid_v = 1.0 / (1.0 + jnp.exp(-hidden))
    return (hidden * sigmoid_v, sigmoid_v * (1.0 + hidden * (1.0 - sigmoid_v)))


def pick_rows(column, size):
    wide = lax.broadcasted_iota(jnp.int32, (column.shape[0], size), 1)
    return jnp.where(wide == column, 1.0, 0.0).astype(BF16)


def drop_rows(row, size):
    tall = lax.broadcasted_iota(jnp.int32, (size, row.shape[1]), 0)
    return jnp.where(tall == row, 1.0, 0.0).astype(BF16)


def as_column(row):
    return jnp.transpose(jnp.broadcast_to(row, (8, row.shape[1])))[:, :1]


def dot(a, b, ca=1, cb=0):
    return lax.dot_general(a, b, (((ca,), (cb,)), ((), ())), preferred_element_type=F32)


def kernel(
    n, fine, wd_hbm, gain, shift, ws_hbm, child, live, send_rows, nbr, gout,
    feat_o, fine_o, down_o, gain_o, shift_o,
    wd, ws, gsend, gpair, conv, table, tgrad, facc, gpre, gppair, crow, dspread, part,
    sbuf, rbuf, obuf, st1, st2, hsend, hrecv, bsend, brecv,
    wsem, pss, psr, s1s, s1r, s2s, s2r, hss, hsr, bss, bsr, rss, rsr, ags, agr,
):
    kd, cin, c = wd.shape
    ks, _, co = ws.shape
    rows = child.shape[1]
    ndir, halo = send_rows.shape
    fine_rows = fine.shape[0]
    ext = rows + ndir * halo
    q_count, half, width = part.shape
    me = lax.axis_index("coarse")
    core = lax.rem(me, 2)
    pair = me + 1 - 2 * core

    wd_copy = pltpu.make_async_copy(wd_hbm, wd, wsem.at[0])
    ws_copy = pltpu.make_async_copy(ws_hbm, ws, wsem.at[1])
    wd_copy.start()
    ws_copy.start()

    barrier = pltpu.get_barrier_semaphore()

    @pl.loop(1, n)
    def _(d):
        pl.semaphore_signal(barrier, inc=1, device_id={"coarse": lax.rem(me + d, n)}, device_id_type=MESH)

    def remote(src, dst, ssem, rsem, to):
        return pltpu.make_async_remote_copy(
            src_ref=src, dst_ref=dst, send_sem=ssem, recv_sem=rsem,
            device_id={"coarse": to}, device_id_type=MESH,
        )

    def tell_all(st, ss, sr):
        @pl.loop(1, n)
        def _(d):
            remote(st.at[me], st.at[me], ss.at[d], sr.at[me], lax.rem(me + d, n)).start()

    def hear_all(st, ss, sr):
        @pl.loop(1, n)
        def _(d):
            src = lax.rem(me - d + n, n)
            remote(st.at[src], st.at[src], ss.at[d], sr.at[src], lax.rem(me + d, n)).wait()

    conv[...] = jnp.zeros_like(conv)
    wd_copy.wait()

    kh = kd // 2

    def children(k):
        sel = pick_rows(as_column(child[pl.ds(k, 1), :]), fine_rows)
        return dot(sel, fine[...]).astype(BF16)

    @pl.loop(0, kh)
    def _(i):
        mine, other = core * kh + i, (1 - core) * kh + i
        g_other = children(other)
        gsend[i] = g_other
        g_mine = children(mine)
        gpair[i, :rows, :] = g_mine
        conv[...] += dot(g_other, wd[other]) + dot(g_mine, wd[mine])

    for k in range(kd):
        crow[:, k * rows : (k + 1) * rows] = child[k : k + 1, :]

    wide = conv[...].astype(BF16).astype(F32)
    conv[...] = wide
    row_mask = (lax.broadcasted_iota(jnp.int32, (rows, 1), 0) < live[0]).astype(F32)
    masked = row_mask * wide
    sums = jnp.sum(masked, 0, keepdims=True)
    squares = jnp.sum(masked * wide, 0, keepdims=True)
    pieces = c // 128
    for r in range(pieces):
        st1[me, r : r + 1, :] = sums[:, r * 128 : (r + 1) * 128]
        st1[me, pieces + r : pieces + r + 1, :] = squares[:, r * 128 : (r + 1) * 128]
    live_count = jnp.full((8, 128), live[0], jnp.int32).astype(F32)
    st1[me, 2 * pieces : 2 * pieces + 8, :] = live_count
    pl.semaphore_wait(barrier, n - 1)
    tell_all(st1, s1s, s1r)
    gath_copy = remote(gsend, gpair.at[:, pl.ds(rows, rows)], pss.at[0], psr.at[0], pair)
    gath_copy.start()

    tgrad[...] = jnp.zeros_like(tgrad)
    ws_copy.wait()

    @pl.loop(0, ks // 3)
    def _(k3):
        total_k = None
        for i in range(3):
            k = k3 * 3 + i
            spread = dot(drop_rows(nbr[pl.ds(k, 1), :], ext), gout[...]).astype(BF16)
            term = dot(spread, ws[k], 1, 1)
            total_k = term if total_k is None else total_k + term
        tgrad[...] += total_k

    def back_copy(j):
        return remote(
            bsend.at[j], brecv.at[j], bss.at[j], bsr.at[j], lax.rem(me - OFFSETS[j] + n, n)
        )

    def halo_copy(j):
        return remote(
            hsend.at[j], hrecv.at[j], hss.at[j], hsr.at[j], lax.rem(me + OFFSETS[j] + n, n)
        )

    for j in range(ndir):
        bsend[j] = tgrad[rows + j * halo : rows + (j + 1) * halo, :].astype(BF16)
        back_copy(j).start()

    hear_all(st1, s1s, s1r)

    def add_slots(st):
        acc = st[0]
        for i in range(1, n):
            acc = acc + st[i]
        return acc

    def flat(acc, first):
        return jnp.concatenate([acc[first + r : first + r + 1, :] for r in range(pieces)], 1)

    acc1 = add_slots(st1)
    filled = acc1[2 * pieces : 2 * pieces + 1, :1]
    mean = flat(acc1, 0) / filled
    variance = flat(acc1, pieces) / filled - mean * mean
    inv_std = lax.rsqrt(variance + EPSILON)
    normed = (conv[...] - mean) * inv_std
    hidden = normed * gain[...] + shift[...]
    activated, slope = silu_parts(hidden)
    active = (row_mask * activated).astype(BF16)
    table[:rows, :] = active
    conv[...] = normed
    for j in range(ndir):
        sel = drop_rows(send_rows[j : j + 1, :], rows)
        hsend[j] = dot(sel, active, 0, 0).astype(BF16)
        halo_copy(j).start()

    grad_active = tgrad[:rows, :]
    for j in range(ndir):
        back_copy(j).wait()
        giver = me + OFFSETS[j]
        there = jnp.logical_and(giver >= 0, giver < n)
        back = jnp.where(there, brecv[j], jnp.zeros_like(brecv[j]))
        grad_active = grad_active + dot(drop_rows(send_rows[j : j + 1, :], rows), back)
    grad_hidden = row_mask * grad_active * slope
    tgrad[:rows, :] = grad_hidden
    part_gain = jnp.sum(grad_hidden * normed, 0, keepdims=True)
    part_shift = jnp.sum(grad_hidden, 0, keepdims=True)
    for r in range(pieces):
        st2[me, r : r + 1, :] = part_gain[:, r * 128 : (r + 1) * 128]
        st2[me, pieces + r : pieces + r + 1, :] = part_shift[:, r * 128 : (r + 1) * 128]
    tell_all(st2, s2s, s2r)

    for j in range(ndir):
        halo_copy(j).wait()
        giver = me - OFFSETS[j]
        there = jnp.logical_and(giver >= 0, giver < n)
        table[rows + j * halo : rows + (j + 1) * halo, :] = jnp.where(
            there, hrecv[j], jnp.zeros_like(hrecv[j])
        )
    facc[...] = jnp.zeros_like(facc)

    def forward(first, last):
        @pl.loop(first, last)
        def _(k):
            term = None
            for i in range(3):
                sel = pick_rows(as_column(nbr[pl.ds(3 * k + i, 1), :]), ext)
                term_i = dot(dot(sel, table[...]).astype(BF16), ws[3 * k + i])
                term = term_i if term is None else term + term_i
            facc[...] += term

    forward(0, 2)

    hear_all(st2, s2s, s2r)
    acc2 = add_slots(st2)
    grad_gain = flat(acc2, 0)
    grad_shift = flat(acc2, pieces)
    gain_o[...] = grad_gain
    shift_o[...] = grad_shift
    pre = (
        row_mask * gain[...] * inv_std
        * (tgrad[:rows, :] - (grad_shift + conv[...] * grad_gain) / filled)
    ).astype(BF16)
    gpre[...] = pre
    gppair[:rows, :] = pre
    gpre_copy = remote(gpre, gppair.at[pl.ds(rows, rows)], pss.at[1], psr.at[1], pair)
    gpre_copy.start()

    def spread_down():
        @pl.loop(0, kd // 4)
        def _(k4):
            for i in range(4):
                k = 4 * k4 + i
                dspread[pl.ds(pl.multiple_of(k * rows, rows), rows), :] = dot(
                    gpre[...], wd[k], 1, 1
                ).astype(BF16)

    spread_down()
    gath_copy.wait()
    gpre_copy.wait()

    masks = []
    while 2 ** (len(masks) + 1) < n:
        masks.append(2 ** (len(masks) + 1))
    steps = len(masks)
    lows, sends, partners, lengths, places = [], [], [], [], []
    low, length, place = 0, half, 0
    for m in masks:
        bit = lax.rem(me // m, 2)
        length = length // 2
        lengths.append(length)
        sends.append(pl.multiple_of(low + (1 - bit) * length, length))
        low = low + bit * length
        lows.append(pl.multiple_of(low, length))
        partners.append(me + m - 2 * m * bit)
        places.append(place)
        place += length
    base = pl.multiple_of(core * half, half)
    stages = 2 * steps + 1

    def sum_copy(q, s):
        span = pl.ds(places[s], lengths[s])
        return remote(
            sbuf.at[q, span], rbuf.at[q, span], rss.at[q, s], rsr.at[q, s], partners[s]
        )

    def full_copy(q, t):
        s = 2 * steps - 1 - t
        if s >= 0:
            span = pl.ds(pl.multiple_of(base + lows[s], lengths[s]), lengths[s])
            to = partners[s]
        else:
            span, to = pl.ds(base, half), pair
        return remote(
            obuf.at[q, span], obuf.at[q, span], ags.at[q, s + 1], agr.at[q, s + 1], to
        )

    def start(q, t):
        if t < steps:
            sbuf[q, places[t] : places[t] + lengths[t], :] = part[
                q, pl.ds(sends[t], lengths[t]), :
            ].astype(BF16)
            sum_copy(q, t).start()
        elif t < stages:
            full_copy(q, t).start()

    def finish(q, t):
        if t < steps:
            sum_copy(q, t).wait()
            span = pl.ds(lows[t], lengths[t])
            summed = part[q, span, :] + rbuf[q, places[t] : places[t] + lengths[t], :].astype(F32)
            if t < steps - 1:
                part[q, span, :] = summed
            else:
                place_o = pl.ds(pl.multiple_of(base + lows[t], lengths[t]), lengths[t])
                obuf[q, place_o, :] = summed.astype(BF16)
        else:
            full_copy(q, t).wait()

    @pl.loop(0, kh)
    def _(i):
        term = dot(gpair[i], gppair[...], 0, 0)
        for q in range(q_count):
            part[q, pl.ds(pl.multiple_of(i * cin, cin), cin), :] = term[
                :, q * width : (q + 1) * width
            ]

    for q in range(q_count):
        start(q, 0)

    tile = 256

    def fine_tiles(first, last):
        @pl.loop(first, last)
        def _(i):
            first_row = pl.multiple_of(i * tile, tile)
            sel = drop_rows(crow[...] - first_row, tile)
            fine_o[pl.ds(first_row, tile), :] = dot(sel, dspread[...]).astype(BF16)

    units = [functools.partial(forward, k, k + 1) for k in range(2, ks // 3)]
    tiles = fine_rows // tile
    units += [functools.partial(fine_tiles, i, i + 1) for i in range(tiles)]
    for t in range(stages):
        for q in range(q_count):
            finish(q, t)
            start(q, t + 1)
            if units:
                units.pop(0)()
    for unit in units:
        unit()
    feat_o[...] = facc[...].astype(BF16)
    for q in range(q_count):
        down_o[:, q * width : (q + 1) * width] = obuf[q]


def copies(*refs):
    count = (len(refs) - 1) // 2
    sem = refs[-1]
    moves = [
        pltpu.make_async_copy(refs[i], refs[count + i], sem.at[i]) for i in range(count)
    ]
    for move in moves:
        move.start()
    for move in moves:
        move.wait()


def hand_over(*arrays):
    hbm = pl.BlockSpec(memory_space=pl.ANY)
    return pl.pallas_call(
        copies,
        out_shape=tuple(jax.ShapeDtypeStruct(a.shape, a.dtype) for a in arrays),
        in_specs=[hbm] * len(arrays),
        out_specs=(hbm,) * len(arrays),
        scratch_shapes=[pltpu.SemaphoreType.DMA((len(arrays),))],
    )(*arrays)


def body(fine_feats, down_weight, gain, shift, subm_weight, child, live, send_rows, nbr, grad_out):
    n = lax.axis_size("coarse")
    fine_rows, cin = fine_feats.shape
    kd, _, c = down_weight.shape
    ks, _, co = subm_weight.shape
    rows = child.shape[1]
    ndir, halo = send_rows.shape
    ext = rows + ndir * halo
    width = c // LANES
    total = kd * cin
    half = total // 2
    steps = (n - 1).bit_length()
    slot = 2 * (c // 128)
    vmem = pl.BlockSpec(memory_space=pltpu.VMEM)
    hbm = pl.BlockSpec(memory_space=pl.ANY)
    smem = pl.BlockSpec(memory_space=pltpu.SMEM)
    dma = pltpu.SemaphoreType.DMA
    features, grad_fine, grad_down, grad_gain, grad_shift = pl.pallas_call(
        functools.partial(kernel, n),
        out_shape=(
            jax.ShapeDtypeStruct((rows, co), BF16),
            jax.ShapeDtypeStruct((fine_rows, cin), BF16),
            jax.ShapeDtypeStruct((total, c), BF16),
            jax.ShapeDtypeStruct((1, c), F32),
            jax.ShapeDtypeStruct((1, c), F32),
        ),
        in_specs=[vmem, hbm, vmem, vmem, hbm, vmem, smem, vmem, vmem, vmem],
        out_specs=(vmem,) * 5,
        scratch_shapes=[
            pltpu.VMEM((kd, cin, c), BF16),
            pltpu.VMEM((ks, c, co), BF16),
            pltpu.VMEM((kd // 2, rows, cin), BF16),
            pltpu.VMEM((kd // 2, 2 * rows, cin), BF16),
            pltpu.VMEM((rows, c), F32),
            pltpu.VMEM((ext, c), BF16),
            pltpu.VMEM((ext, c), F32),
            pltpu.VMEM((rows, co), F32),
            pltpu.VMEM((rows, c), BF16),
            pltpu.VMEM((2 * rows, c), BF16),
            pltpu.VMEM((1, kd * rows), jnp.int32),
            pltpu.VMEM((kd * rows, cin), BF16),
            pltpu.VMEM((LANES, half, width), F32),
            pltpu.VMEM((LANES, half, width), BF16),
            pltpu.VMEM((LANES, half, width), BF16),
            pltpu.VMEM((LANES, total, width), BF16),
            pltpu.VMEM((n, slot + 8, 128), F32),
            pltpu.VMEM((n, slot, 128), F32),
            pltpu.VMEM((ndir, halo, c), BF16),
            pltpu.VMEM((ndir, halo, c), BF16),
            pltpu.VMEM((ndir, halo, c), BF16),
            pltpu.VMEM((ndir, halo, c), BF16),
            dma((2,)), dma((2,)), dma((2,)),
            dma((n,)), dma((n,)), dma((n,)), dma((n,)),
            dma((ndir,)), dma((ndir,)), dma((ndir,)), dma((ndir,)),
            dma((LANES, steps)), dma((LANES, steps)), dma((LANES, steps)), dma((LANES, steps)),
        ],
        compiler_params=pltpu.CompilerParams(
            collective_id=0, has_side_effects=True, vmem_limit_bytes=56 * 1024 * 1024
        ),
    )(
        fine_feats, down_weight, gain.reshape(1, c), shift.reshape(1, c), subm_weight,
        child, live, send_rows, nbr, grad_out,
    )
    features, grad_fine, grad_down = hand_over(features, grad_fine, grad_down)
    return (
        features,
        grad_fine,
        grad_down.reshape(kd, cin, c),
        grad_gain.reshape(c),
        grad_shift.reshape(c),
    )


def solution(mesh):
    in_specs = (
        P(("groups", "coarse"), None),
        P(),
        P(),
        P(),
        P(),
        P("groups", "coarse"),
        P(("groups", "coarse")),
        P("groups", "coarse"),
        P("groups", "coarse"),
        P(("groups", "coarse"), None),
    )
    out_specs = (
        P(("groups", "coarse"), None),
        P(("groups", "coarse"), None),
        P("groups", None, None),
        P("groups"),
        P("groups"),
    )
    return jax.shard_map(body, mesh=mesh, in_specs=in_specs, out_specs=out_specs, check_vma=False)
```

```python
import functools

import jax
import jax.numpy as jnp
from jax import lax
from jax.experimental import pallas as pl
from jax.experimental.pallas import tpu as pltpu
from jax.sharding import PartitionSpec as P

OFFSETS = (1, 2, -1, -2)
EPSILON = 1e-05
LANES = 4
F32 = jnp.float32
BF16 = jnp.bfloat16
MESH = pl.DeviceIdType.MESH


def silu_parts(hidden):
    sigmoid_v = 1.0 / (1.0 + jnp.exp(-hidden))
    return (hidden * sigmoid_v, sigmoid_v * (1.0 + hidden * (1.0 - sigmoid_v)))


def pick_rows(column, size):
    wide = lax.broadcasted_iota(jnp.int32, (column.shape[0], size), 1)
    return jnp.where(wide == column, 1.0, 0.0).astype(BF16)


def drop_rows(row, size):
    tall = lax.broadcasted_iota(jnp.int32, (size, row.shape[1]), 0)
    return jnp.where(tall == row, 1.0, 0.0).astype(BF16)


def as_column(row):
    return jnp.transpose(jnp.broadcast_to(row, (8, row.shape[1])))[:, :1]


def dot(a, b, ca=1, cb=0):
    return lax.dot_general(a, b, (((ca,), (cb,)), ((), ())), preferred_element_type=F32)


def kernel(
    n, fine, wd_hbm, gain, shift, ws_hbm, child, live, send_rows, nbr, gout,
    feat_o, fine_o, down_o, gain_o, shift_o,
    wd, ws, gsend, gpair, conv, table, tgrad, facc, gpre, gppair, crow, dspread, part,
    sbuf, rbuf, obuf, st1, st2, hsend, hrecv, bsend, brecv,
    wsem, pss, psr, s1s, s1r, s2s, s2r, hss, hsr, bss, bsr, rss, rsr, ags, agr,
):
    kd, cin, c = wd.shape
    ks, _, co = ws.shape
    rows = child.shape[1]
    ndir, halo = send_rows.shape
    fine_rows = fine.shape[0]
    ext = rows + ndir * halo
    q_count, half, width = part.shape
    me = lax.axis_index("coarse")
    core = lax.rem(me, 2)
    pair = me + 1 - 2 * core

    wd_copy = pltpu.make_async_copy(wd_hbm, wd, wsem.at[0])
    ws_copy = pltpu.make_async_copy(ws_hbm, ws, wsem.at[1])
    wd_copy.start()
    ws_copy.start()

    barrier = pltpu.get_barrier_semaphore()

    @pl.loop(1, n)
    def _(d):
        pl.semaphore_signal(barrier, inc=1, device_id={"coarse": lax.rem(me + d, n)}, device_id_type=MESH)

    def remote(src, dst, ssem, rsem, to):
        return pltpu.make_async_remote_copy(
            src_ref=src, dst_ref=dst, send_sem=ssem, recv_sem=rsem,
            device_id={"coarse": to}, device_id_type=MESH,
        )

    def tell_all(st, ss, sr):
        @pl.loop(1, n)
        def _(d):
            remote(st.at[me], st.at[me], ss.at[d], sr.at[me], lax.rem(me + d, n)).start()

    def hear_all(st, ss, sr):
        @pl.loop(1, n)
        def _(d):
            src = lax.rem(me - d + n, n)
            remote(st.at[src], st.at[src], ss.at[d], sr.at[src], lax.rem(me + d, n)).wait()

    conv[...] = jnp.zeros_like(conv)
    wd_copy.wait()

    kh = kd // 2

    def children(k):
        sel = pick_rows(as_column(child[pl.ds(k, 1), :]), fine_rows)
        return dot(sel, fine[...]).astype(BF16)

    @pl.loop(0, kh)
    def _(i):
        mine, other = core * kh + i, (1 - core) * kh + i
        g_other = children(other)
        gsend[i] = g_other
        g_mine = children(mine)
        gpair[i, :rows, :] = g_mine
        conv[...] += dot(g_other, wd[other]) + dot(g_mine, wd[mine])

    for k in range(kd):
        crow[:, k * rows : (k + 1) * rows] = child[k : k + 1, :]

    wide = conv[...].astype(BF16).astype(F32)
    conv[...] = wide
    row_mask = (lax.broadcasted_iota(jnp.int32, (rows, 1), 0) < live[0]).astype(F32)
    masked = row_mask * wide
    sums = jnp.sum(masked, 0, keepdims=True)
    squares = jnp.sum(masked * wide, 0, keepdims=True)
    pieces = c // 128
    for r in range(pieces):
        st1[me, r : r + 1, :] = sums[:, r * 128 : (r + 1) * 128]
        st1[me, pieces + r : pieces + r + 1, :] = squares[:, r * 128 : (r + 1) * 128]
    live_count = jnp.full((8, 128), live[0], jnp.int32).astype(F32)
    st1[me, 2 * pieces : 2 * pieces + 8, :] = live_count
    pl.semaphore_wait(barrier, n - 1)
    tell_all(st1, s1s, s1r)
    gath_copy = remote(gsend, gpair.at[:, pl.ds(rows, rows)], pss.at[0], psr.at[0], pair)
    gath_copy.start()

    tgrad[...] = jnp.zeros_like(tgrad)
    ws_copy.wait()

    @pl.loop(0, ks // 3)
    def _(k3):
        total_k = None
        for i in range(3):
            k = k3 * 3 + i
            spread = dot(drop_rows(nbr[pl.ds(k, 1), :], ext), gout[...]).astype(BF16)
            term = dot(spread, ws[k], 1, 1)
            total_k = term if total_k is None else total_k + term
        tgrad[...] += total_k

    def back_copy(j):
        return remote(
            bsend.at[j], brecv.at[j], bss.at[j], bsr.at[j], lax.rem(me - OFFSETS[j] + n, n)
        )

    def halo_copy(j):
        return remote(
            hsend.at[j], hrecv.at[j], hss.at[j], hsr.at[j], lax.rem(me + OFFSETS[j] + n, n)
        )

    for j in range(ndir):
        bsend[j] = tgrad[rows + j * halo : rows + (j + 1) * halo, :].astype(BF16)
        back_copy(j).start()

    hear_all(st1, s1s, s1r)

    def add_slots(st):
        acc = st[0]
        for i in range(1, n):
            acc = acc + st[i]
        return acc

    def flat(acc, first):
        return jnp.concatenate([acc[first + r : first + r + 1, :] for r in range(pieces)], 1)

    acc1 = add_slots(st1)
    filled = acc1[2 * pieces : 2 * pieces + 1, :1]
    mean = flat(acc1, 0) / filled
    variance = flat(acc1, pieces) / filled - mean * mean
    inv_std = lax.rsqrt(variance + EPSILON)
    normed = (conv[...] - mean) * inv_std
    hidden = normed * gain[...] + shift[...]
    activated, slope = silu_parts(hidden)
    active = (row_mask * activated).astype(BF16)
    table[:rows, :] = active
    conv[...] = normed
    for j in range(ndir):
        sel = drop_rows(send_rows[j : j + 1, :], rows)
        hsend[j] = dot(sel, active, 0, 0).astype(BF16)
        halo_copy(j).start()

    grad_active = tgrad[:rows, :]
    for j in range(ndir):
        back_copy(j).wait()
        giver = me + OFFSETS[j]
        there = jnp.logical_and(giver >= 0, giver < n)
        back = jnp.where(there, brecv[j], jnp.zeros_like(brecv[j]))
        grad_active = grad_active + dot(drop_rows(send_rows[j : j + 1, :], rows), back)
    grad_hidden = row_mask * grad_active * slope
    tgrad[:rows, :] = grad_hidden
    part_gain = jnp.sum(grad_hidden * normed, 0, keepdims=True)
    part_shift = jnp.sum(grad_hidden, 0, keepdims=True)
    for r in range(pieces):
        st2[me, r : r + 1, :] = part_gain[:, r * 128 : (r + 1) * 128]
        st2[me, pieces + r : pieces + r + 1, :] = part_shift[:, r * 128 : (r + 1) * 128]
    tell_all(st2, s2s, s2r)

    for j in range(ndir):
        halo_copy(j).wait()
        giver = me - OFFSETS[j]
        there = jnp.logical_and(giver >= 0, giver < n)
        table[rows + j * halo : rows + (j + 1) * halo, :] = jnp.where(
            there, hrecv[j], jnp.zeros_like(hrecv[j])
        )
    facc[...] = jnp.zeros_like(facc)

    def forward(first, last):
        @pl.loop(first, last)
        def _(k):
            term = None
            for i in range(3):
                sel = pick_rows(as_column(nbr[pl.ds(3 * k + i, 1), :]), ext)
                term_i = dot(dot(sel, table[...]).astype(BF16), ws[3 * k + i])
                term = term_i if term is None else term + term_i
            facc[...] += term

    forward(0, 2)

    hear_all(st2, s2s, s2r)
    acc2 = add_slots(st2)
    grad_gain = flat(acc2, 0)
    grad_shift = flat(acc2, pieces)
    gain_o[...] = grad_gain
    shift_o[...] = grad_shift
    pre = (
        row_mask * gain[...] * inv_std
        * (tgrad[:rows, :] - (grad_shift + conv[...] * grad_gain) / filled)
    ).astype(BF16)
    gpre[...] = pre
    gppair[:rows, :] = pre
    gpre_copy = remote(gpre, gppair.at[pl.ds(rows, rows)], pss.at[1], psr.at[1], pair)
    gpre_copy.start()

    def spread_down():
        @pl.loop(0, kd // 4)
        def _(k4):
            for i in range(4):
                k = 4 * k4 + i
                dspread[pl.ds(pl.multiple_of(k * rows, rows), rows), :] = dot(
                    gpre[...], wd[k], 1, 1
                ).astype(BF16)

    spread_down()
    gath_copy.wait()
    gpre_copy.wait()

    masks = []
    while 2 ** (len(masks) + 1) < n:
        masks.append(2 ** (len(masks) + 1))
    steps = len(masks)
    lows, sends, partners, lengths, places = [], [], [], [], []
    low, length, place = 0, half, 0
    for m in masks:
        bit = lax.rem(me // m, 2)
        length = length // 2
        lengths.append(length)
        sends.append(pl.multiple_of(low + (1 - bit) * length, length))
        low = low + bit * length
        lows.append(pl.multiple_of(low, length))
        partners.append(me + m - 2 * m * bit)
        places.append(place)
        place += length
    base = pl.multiple_of(core * half, half)
    stages = 2 * steps + 1

    def sum_copy(q, s):
        span = pl.ds(places[s], lengths[s])
        return remote(
            sbuf.at[q, span], rbuf.at[q, span], rss.at[q, s], rsr.at[q, s], partners[s]
        )

    def full_copy(q, t):
        s = 2 * steps - 1 - t
        if s >= 0:
            span = pl.ds(pl.multiple_of(base + lows[s], lengths[s]), lengths[s])
            to = partners[s]
        else:
            span, to = pl.ds(base, half), pair
        return remote(
            obuf.at[q, span], obuf.at[q, span], ags.at[q, s + 1], agr.at[q, s + 1], to
        )

    def start(q, t):
        if t < steps:
            sbuf[q, places[t] : places[t] + lengths[t], :] = part[
                q, pl.ds(sends[t], lengths[t]), :
            ].astype(BF16)
            sum_copy(q, t).start()
        elif t < stages:
            full_copy(q, t).start()

    def finish(q, t):
        if t < steps:
            sum_copy(q, t).wait()
            span = pl.ds(lows[t], lengths[t])
            summed = part[q, span, :] + rbuf[q, places[t] : places[t] + lengths[t], :].astype(F32)
            if t < steps - 1:
                part[q, span, :] = summed
            else:
                place_o = pl.ds(pl.multiple_of(base + lows[t], lengths[t]), lengths[t])
                obuf[q, place_o, :] = summed.astype(BF16)
        else:
            full_copy(q, t).wait()

    @pl.loop(0, kh)
    def _(i):
        term = dot(gpair[i], gppair[...], 0, 0)
        for q in range(q_count):
            part[q, pl.ds(pl.multiple_of(i * cin, cin), cin), :] = term[
                :, q * width : (q + 1) * width
            ]

    for q in range(q_count):
        start(q, 0)

    tile = 256

    def fine_tiles(first, last):
        @pl.loop(first, last)
        def _(i):
            first_row = pl.multiple_of(i * tile, tile)
            sel = drop_rows(crow[...] - first_row, tile)
            fine_o[pl.ds(first_row, tile), :] = dot(sel, dspread[...]).astype(BF16)

    units = [functools.partial(forward, k, k + 1) for k in range(2, ks // 3)]
    tiles = fine_rows // tile
    units += [functools.partial(fine_tiles, i, i + 1) for i in range(tiles)]
    events = stages * q_count
    done = 0
    for event in range(events):
        t, q = event // q_count, event % q_count
        finish(q, t)
        start(q, t + 1)
        due = (event + 1) * len(units) // events
        for unit in units[done:due]:
            unit()
        done = due
    feat_o[...] = facc[...].astype(BF16)
    for q in range(q_count):
        down_o[:, q * width : (q + 1) * width] = obuf[q]


def copies(*refs):
    count = len(refs) // 2
    for i in range(count):
        refs[count + i][...] = refs[i][...]


def hand_over(parts, *arrays):
    specs = [pl.BlockSpec((a.shape[0] // parts, a.shape[1]), lambda i: (i, 0)) for a in arrays]
    return pl.pallas_call(
        copies,
        grid=(parts,),
        out_shape=tuple(jax.ShapeDtypeStruct(a.shape, a.dtype) for a in arrays),
        in_specs=specs,
        out_specs=tuple(specs),
    )(*arrays)


def body(fine_feats, down_weight, gain, shift, subm_weight, child, live, send_rows, nbr, grad_out):
    n = lax.axis_size("coarse")
    fine_rows, cin = fine_feats.shape
    kd, _, c = down_weight.shape
    ks, _, co = subm_weight.shape
    rows = child.shape[1]
    ndir, halo = send_rows.shape
    ext = rows + ndir * halo
    width = c // LANES
    total = kd * cin
    half = total // 2
    steps = (n - 1).bit_length()
    slot = 2 * (c // 128)
    vmem = pl.BlockSpec(memory_space=pltpu.VMEM)
    hbm = pl.BlockSpec(memory_space=pl.ANY)
    smem = pl.BlockSpec(memory_space=pltpu.SMEM)
    dma = pltpu.SemaphoreType.DMA
    features, grad_fine, grad_down, grad_gain, grad_shift = pl.pallas_call(
        functools.partial(kernel, n),
        out_shape=(
            jax.ShapeDtypeStruct((rows, co), BF16),
            jax.ShapeDtypeStruct((fine_rows, cin), BF16),
            jax.ShapeDtypeStruct((total, c), BF16),
            jax.ShapeDtypeStruct((1, c), F32),
            jax.ShapeDtypeStruct((1, c), F32),
        ),
        in_specs=[vmem, hbm, vmem, vmem, hbm, vmem, smem, vmem, vmem, vmem],
        out_specs=(vmem,) * 5,
        scratch_shapes=[
            pltpu.VMEM((kd, cin, c), BF16),
            pltpu.VMEM((ks, c, co), BF16),
            pltpu.VMEM((kd // 2, rows, cin), BF16),
            pltpu.VMEM((kd // 2, 2 * rows, cin), BF16),
            pltpu.VMEM((rows, c), F32),
            pltpu.VMEM((ext, c), BF16),
            pltpu.VMEM((ext, c), F32),
            pltpu.VMEM((rows, co), F32),
            pltpu.VMEM((rows, c), BF16),
            pltpu.VMEM((2 * rows, c), BF16),
            pltpu.VMEM((1, kd * rows), jnp.int32),
            pltpu.VMEM((kd * rows, cin), BF16),
            pltpu.VMEM((LANES, half, width), F32),
            pltpu.VMEM((LANES, half, width), BF16),
            pltpu.VMEM((LANES, half, width), BF16),
            pltpu.VMEM((LANES, total, width), BF16),
            pltpu.VMEM((n, slot + 8, 128), F32),
            pltpu.VMEM((n, slot, 128), F32),
            pltpu.VMEM((ndir, halo, c), BF16),
            pltpu.VMEM((ndir, halo, c), BF16),
            pltpu.VMEM((ndir, halo, c), BF16),
            pltpu.VMEM((ndir, halo, c), BF16),
            dma((2,)), dma((2,)), dma((2,)),
            dma((n,)), dma((n,)), dma((n,)), dma((n,)),
            dma((ndir,)), dma((ndir,)), dma((ndir,)), dma((ndir,)),
            dma((LANES, steps)), dma((LANES, steps)), dma((LANES, steps)), dma((LANES, steps)),
        ],
        compiler_params=pltpu.CompilerParams(
            collective_id=0, has_side_effects=True, vmem_limit_bytes=56 * 1024 * 1024
        ),
    )(
        fine_feats, down_weight, gain.reshape(1, c), shift.reshape(1, c), subm_weight,
        child, live, send_rows, nbr, grad_out,
    )
    features, grad_fine, grad_down = hand_over(4, features, grad_fine, grad_down)
    return (
        features,
        grad_fine,
        grad_down.reshape(kd, cin, c),
        grad_gain.reshape(c),
        grad_shift.reshape(c),
    )


def solution(mesh):
    in_specs = (
        P(("groups", "coarse"), None),
        P(),
        P(),
        P(),
        P(),
        P("groups", "coarse"),
        P(("groups", "coarse")),
        P("groups", "coarse"),
        P("groups", "coarse"),
        P(("groups", "coarse"), None),
    )
    out_specs = (
        P(("groups", "coarse"), None),
        P(("groups", "coarse"), None),
        P("groups", None, None),
        P("groups"),
        P("groups"),
    )
    return jax.shard_map(body, mesh=mesh, in_specs=in_specs, out_specs=out_specs, check_vma=False)
```
